32 devices in a mesh: leaf: 4 (over z), sub: 8 (over y, x, core).
Axes of the slice: x: 2, y: 2, z: 4, core: 2. Of those that a mesh axis runs over, the one named last changes fastest.
Arguments:
- right_side: float32 [65536, 256], P(('leaf', 'sub')), may hold values from -6 to 6
- u_bases: float32 [4, 65536, 256], P(None, ('leaf', 'sub')), may hold values from -6 to 6
- v_bases: float32 [4, 65536, 256], P(None, ('leaf', 'sub')), may hold values from -0.00271875 to 0.00271875
Outputs:
- solution: float32 [65536, 256], P(('leaf', 'sub'))
The draws below stay inside these ranges and needn't reach their ends.
All inputs are finite; a program needn't handle non-finite values.
Results may differ from the reference program's by a relative error of at most 0.00022.
Values sent between devices are 32-bit elements; how exact they have to be, the bound alone decides.
A program may use at most 128 MiB of HBM per device.

```python
import math
import jax
import jax.numpy as jnp
from jax import lax

R = 256
NRHS = 256
LEVELS = 4
N_ROWS = 65536


def draw_v_bases(key, part):
    key_entries, key_rows = jax.random.split(key)
    entries = jax.random.truncated_normal(key_entries, -4.0, 4.0, (LEVELS, N_ROWS, R), jnp.float32)
    spread = 1.15
    row_log = jax.random.uniform(key_rows, (LEVELS, N_ROWS, 1), jnp.float32, -spread, spread)
    row_scale = jnp.exp(row_log) / math.sqrt(math.sinh(2.0 * spread) / (2.0 * spread))
    levels_axis = jnp.arange(LEVELS).astype(jnp.float32)
    level_scale = 0.32 / math.sqrt(R) * jnp.sqrt(2.0 ** (levels_axis + 1.0) / N_ROWS)
    return entries * row_scale * level_scale.reshape(LEVELS, 1, 1)


def block_levels(stream_key, dims, pieces, smallest, high):
    loudness = 1.0
    for dim, shards_of in pieces:
        heights = jax.random.uniform(jax.random.fold_in(jax.random.fold_in(stream_key, 6), dim), (shards_of,), jnp.float32, smallest / len(pieces), high / len(pieces))
        loudness = loudness * jnp.repeat(jnp.exp(heights), dims[dim] // shards_of).reshape((-1,) + (1,) * (len(dims) - 1 - dim))
    return loudness


def centred(rng, dims, width, most, cuts=(), kind=jnp.bfloat16):
    drawn = jax.random.normal(rng, dims, jnp.float32) * width
    if len(cuts) > 0:
        drawn = block_levels(rng, dims, cuts, -0.22, 0.18) * drawn
    return jnp.clip(drawn, min=-most, max=most).astype(kind)


def setup_inputs(seed: int = 0) -> dict:
    streams_of = jax.random.split(jax.random.key(seed), 4)
    return {
        "right_side": centred(streams_of[0], (N_ROWS, NRHS), 1.0, 6.0, ((0, 32),), jnp.float32),
        "u_bases": centred(streams_of[1], (LEVELS, N_ROWS, R), 1.0, 6.0, ((1, 32),), jnp.float32),
        "v_bases": draw_v_bases(jax.random.fold_in(streams_of[3], 71), 0),
    }


def reference(right_side, u_bases, v_bases):
    total_rows = right_side.shape[0]
    stacked = jnp.concatenate([right_side] + [u_bases[basis_index] for basis_index in range(LEVELS)], axis=1)
    for level_index in range(LEVELS - 1, -1, -1):
        children = 2 ** (level_index + 1)
        child_rows = total_rows // children
        width_used = NRHS + level_index * R
        blocks = stacked[:, :width_used + R].reshape(children, child_rows, width_used + R)
        v_blocks = v_bases[level_index].reshape(children, child_rows, R)
        sums = jnp.einsum('cnr,cnk->crk', v_blocks, blocks, precision=lax.Precision.HIGHEST)
        pairs = sums.reshape(children // 2, 2, R, width_used + R)
        first_sums = pairs[:, 0]
        second_sums = pairs[:, 1]
        identity = jnp.broadcast_to(jnp.eye(R, dtype=jnp.float32), (children // 2, R, R))
        upper = jnp.concatenate([identity, second_sums[:, :, width_used:]], axis=2)
        lower = jnp.concatenate([first_sums[:, :, width_used:], identity], axis=2)
        system = jnp.concatenate([upper, lower], axis=1)
        right_terms = jnp.concatenate([second_sums[:, :, :width_used], first_sums[:, :, :width_used]], axis=1)
        answer = jnp.linalg.solve(system, right_terms)
        answer = answer.reshape(children, R, width_used)
        basis = stacked[:, width_used:width_used + R].reshape(children, child_rows, R)
        correction = jnp.einsum('cnr,cru->cnu', basis, answer, precision=lax.Precision.HIGHEST)
        correction = correction.reshape(total_rows, width_used)
        stacked = jnp.concatenate([stacked[:, :width_used] - correction, stacked[:, width_used:]], axis=1)
    return stacked[:, :NRHS]
```

```python
import functools

import jax
import jax.numpy as jnp
from jax import lax
from jax.experimental import pallas as pl
from jax.experimental.pallas import tpu as pltpu
from jax.sharding import PartitionSpec as P

AXES = ("leaf", "sub")
F32 = jnp.float32
VMEM_LIMIT = 56 * 1024 * 1024
SETTLED = 4e-6
MOST_SWEEPS = 12


def split(x):
    high = x.astype(jnp.bfloat16)
    return high, (x - high.astype(F32)).astype(jnp.bfloat16)


def dot(a, b):
    return jnp.dot(a, b, preferred_element_type=F32)


def mm(a, b):
    a_high, a_low = split(a)
    b_high, b_low = split(b)
    return dot(a_high, b_high) + (dot(a_high, b_low) + dot(a_low, b_high))


def joined(parity, mine, other):
    first = jnp.where(parity == 0, mine, other)
    second = jnp.where(parity == 0, other, mine)
    return jnp.concatenate([first, second], axis=1)


def gram_kernel(par_ref, v_ref, b_ref, u_ref, mine_ref, other_ref, acc):
    step = pl.program_id(0)
    levels, _, rank = v_ref.shape
    half = rank // 2

    @pl.when(step == 0)
    def _():
        acc[...] = jnp.zeros_like(acc)

    stacked = []
    for j in range(u_ref.shape[0] + 1):
        high, low = split(b_ref[...] if j == 0 else u_ref[j - 1])
        stacked.append(jnp.concatenate([high, low, high], axis=0))
    for k in range(levels):
        high, low = split(v_ref[k])
        rows = jnp.concatenate([high, high, low], axis=0).T
        for j, block in enumerate(stacked):
            product = dot(rows, block)
            place = (pl.ds(k * rank, rank), pl.ds(j * half, half))
            acc[(0,) + place] += product[:, :half]
            acc[(1,) + place] += product[:, half:]

    @pl.when(step == pl.num_programs(0) - 1)
    def _():
        mine_ref[...] = acc[par_ref[0]]
        other_ref[...] = acc[1 - par_ref[0]]


def gram(parity, v, b, u, first, levels, tile):
    level_count, rows, rank = u.shape
    width = (level_count + 1) * rank // 2
    shape = jax.ShapeDtypeStruct((levels * rank, width), F32)
    whole = pl.BlockSpec((levels * rank, width), lambda i: (0, 0))
    return pl.pallas_call(
        gram_kernel,
        grid=(rows // tile,),
        out_shape=(shape, shape),
        in_specs=[
            pl.BlockSpec(memory_space=pltpu.SMEM),
            pl.BlockSpec((levels, tile, rank), lambda i: (first // levels, i, 0)),
            pl.BlockSpec((tile, rank), lambda i: (i, 0)),
            pl.BlockSpec((level_count, tile, rank), lambda i: (0, i, 0)),
        ],
        out_specs=(whole, whole),
        scratch_shapes=[pltpu.VMEM((2, levels * rank, width), F32)],
        compiler_params=pltpu.CompilerParams(vmem_limit_bytes=VMEM_LIMIT),
        cost_estimate=pl.CostEstimate(
            flops=12 * levels * rank * width * rows,
            bytes_accessed=4 * rows * rank * (levels + level_count + 1) + 8 * levels * rank * width,
            transcendentals=0,
        ),
    )(parity, v, b, u)


def solve_values(parity, own_ref, sib_ref, own_other_ref, sib_other_ref):
    half = own_other_ref.shape[1]
    width = own_ref.shape[1] - half
    own_rank = joined(parity, own_ref[:, width:], own_other_ref[...])
    sib_rank = joined(parity, sib_ref[:, width:], sib_other_ref[...])
    terms = sib_ref[:, :width] - mm(sib_rank, own_ref[:, :width])
    power = mm(sib_rank, own_rank)
    answer = terms + mm(power, terms)

    def going(state):
        count, size, _, _ = state
        return jnp.logical_and(size > SETTLED, count < MOST_SWEEPS)

    def sweep(state):
        count, _, power, answer = state
        power = mm(power, power)
        answer = answer + mm(power, answer)
        return count + 1, jnp.sum(power * power), power, answer

    state = (jnp.int32(1), jnp.sum(power * power), power, answer)
    return lax.while_loop(going, sweep, state)[3]


def solve_kernel(par_ref, own_ref, sib_ref, own_other_ref, sib_other_ref, row_ref, col_ref, col_other_ref, z_ref, next_ref):
    parity = par_ref[0]
    answer = solve_values(parity, own_ref, sib_ref, own_other_ref, sib_other_ref)
    z_ref[...] = answer
    column = joined(parity, col_ref[...], col_other_ref[...])
    next_ref[...] = row_ref[...] - mm(column, answer)


def top_kernel(count, par_ref, own_ref, sib_ref, own_other_ref, sib_other_ref, *refs):
    parity = par_ref[0]
    z_refs, z_other_refs, out_ref = refs[:count], refs[count : 2 * count], refs[-1]
    rank = own_ref.shape[0]
    half = own_other_ref.shape[1]
    weights = [solve_values(parity, own_ref, sib_ref, own_other_ref, sib_other_ref)]
    for k in range(1, count + 1):
        weight = z_refs[k - 1][:, :half]
        for j in range(k):
            mine = z_refs[k - 1][:, (j + 1) * half : (j + 2) * half]
            other = z_other_refs[k - 1][:, j * half : (j + 1) * half]
            weight = weight - mm(joined(parity, mine, other), weights[j])
        weights.append(weight)
    for k, weight in enumerate(weights):
        out_ref[k * rank : (k + 1) * rank, :] = weight


def small_call(kernel, shapes, parity, *arrays):
    specs = [pl.BlockSpec(memory_space=pltpu.VMEM)]
    return pl.pallas_call(
        kernel,
        out_shape=shapes,
        in_specs=[pl.BlockSpec(memory_space=pltpu.SMEM)] + specs * len(arrays),
        out_specs=jax.tree.map(lambda _: specs[0], shapes),
        compiler_params=pltpu.CompilerParams(vmem_limit_bytes=VMEM_LIMIT),
        cost_estimate=pl.CostEstimate(flops=3 * 10**9, bytes_accessed=4 * 10**6, transcendentals=0),
    )(parity, *arrays)


def apply_kernel(par_ref, b_ref, u_ref, w_ref, w_other_ref, out_ref, high, low):
    levels, _, rank = u_ref.shape

    @pl.when(pl.program_id(0) == 0)
    def _():
        high[...], low[...] = split(joined(par_ref[0], w_ref[...], w_other_ref[...]))

    total = b_ref[...]
    for k in range(levels):
        u_high, u_low = split(u_ref[k])
        rows = pl.ds(k * rank, rank)
        total = total - (
            dot(u_high, high[rows, :]) + (dot(u_high, low[rows, :]) + dot(u_low, high[rows, :]))
        )
    out_ref[...] = total


def apply(parity, b, u, w, w_other, tile):
    levels, rows, rank = u.shape
    width = b.shape[1]
    half = pl.BlockSpec(w.shape, lambda i: (0, 0))
    return pl.pallas_call(
        apply_kernel,
        grid=(rows // tile,),
        out_shape=jax.ShapeDtypeStruct(b.shape, F32),
        in_specs=[
            pl.BlockSpec(memory_space=pltpu.SMEM),
            pl.BlockSpec((tile, width), lambda i: (i, 0)),
            pl.BlockSpec((levels, tile, rank), lambda i: (0, i, 0)),
            half,
            half,
        ],
        out_specs=pl.BlockSpec((tile, width), lambda i: (i, 0)),
        scratch_shapes=[pltpu.VMEM((levels * rank, width), jnp.bfloat16)] * 2,
        compiler_params=pltpu.CompilerParams(vmem_limit_bytes=VMEM_LIMIT),
    )(parity, b, u, w, w_other)


def swap(block, even_bit, odd_bit):
    count = lax.axis_size(AXES)
    route = [(i, i ^ (1 << (odd_bit if i & 1 else even_bit))) for i in range(count)]
    return lax.ppermute(block, AXES, route)


def local(b, u, v):
    depth = lax.axis_size(AXES).bit_length() - 1
    levels, row_count, rank = u.shape
    half = rank // 2
    tile = min(512, row_count)
    parity = (lax.axis_index(AXES) & 1).reshape(1)

    top, top_other = gram(parity, v, b, u, levels - 1, 1, tile)
    low, low_other = gram(parity, v, b, u, 0, levels - 1, tile)
    top = top + swap(top_other, 0, 0)
    low = low + swap(low_other, 0, 0)
    rows = [low[k * rank : (k + 1) * rank] for k in range(levels - 1)] + [top]

    answers, answers_other = [None] * levels, [None] * levels
    for k in range(levels - 1, -1, -1):
        width = (k + 1) * half
        sibling = depth - 1 - k
        own = rows[k][:, : width + half]
        for step in range(1, sibling):
            own = own + swap(own, step, step % (sibling - 1) + 1)
        sib = swap(own, sibling, sibling)
        own_other = swap(own[:, width:], 0, 0)
        sib_other = swap(sib[:, width:], 0, 0)
        if k > 0:
            cols = jnp.concatenate([rows[i][:, width : width + half] for i in range(k)], axis=0)
            cols_other = swap(cols, 0, 0)
            last = slice((k - 1) * rank, k * rank)
            shape = jax.ShapeDtypeStruct((rank, width), F32)
            z, following = small_call(
                solve_kernel, (shape, shape), parity, own, sib, own_other, sib_other,
                rows[k - 1][:, :width], cols[last], cols_other[last],
            )
            answers[k] = z
            answers_other[k] = swap(z[:, half:], 0, 0)
            rows[k - 1] = following
            if k > 1:
                before = slice(0, (k - 1) * rank)
                column = joined(parity[0], cols[before], cols_other[before])
                change = jnp.dot(column, z, precision=lax.Precision.HIGH, preferred_element_type=F32)
                for i in range(k - 1):
                    rows[i] = rows[i][:, :width] - change[i * rank : (i + 1) * rank]
        else:
            shape = jax.ShapeDtypeStruct((levels * rank, half), F32)
            weights = small_call(
                functools.partial(top_kernel, levels - 1), shape, parity, own, sib, own_other, sib_other,
                *answers[1:], *answers_other[1:],
            )
    return apply(parity, b, u, weights, swap(weights, 0, 0), tile)


def solution(mesh):
    return jax.shard_map(
        local,
        mesh=mesh,
        in_specs=(P(AXES, None), P(None, AXES, None), P(None, AXES, None)),
        out_specs=P(AXES, None),
        check_vma=False,
    )
```

```python
import functools

import jax
import jax.numpy as jnp
from jax import lax
from jax.experimental import pallas as pl
from jax.experimental.pallas import tpu as pltpu
from jax.sharding import PartitionSpec as P

AXES = ("leaf", "sub")
F32 = jnp.float32
VMEM_LIMIT = 56 * 1024 * 1024
SETTLED = 4e-6
MOST_SWEEPS = 12


def split(x):
    high = x.astype(jnp.bfloat16)
    return high, (x - high.astype(F32)).astype(jnp.bfloat16)


def dot(a, b):
    return jnp.dot(a, b, preferred_element_type=F32)


def mm(a, b):
    a_high, a_low = split(a)
    b_high, b_low = split(b)
    return dot(a_high, b_high) + (dot(a_high, b_low) + dot(a_low, b_high))


def joined(parity, mine, other):
    first = jnp.where(parity == 0, mine, other)
    second = jnp.where(parity == 0, other, mine)
    return jnp.concatenate([first, second], axis=1)


def gram_kernel(par_ref, v_ref, b_ref, u_ref, mine_ref, other_ref, acc):
    step = pl.program_id(0)
    levels, _, rank = v_ref.shape
    half = rank // 2

    @pl.when(step == 0)
    def _():
        acc[...] = jnp.zeros_like(acc)

    stacked = []
    for j in range(u_ref.shape[0] + 1):
        high, low = split(b_ref[...] if j == 0 else u_ref[j - 1])
        stacked.append((high, low))
    for k in range(levels):
        high, low = split(v_ref[k].T)
        for j, (block_high, block_low) in enumerate(stacked):
            product = dot(high, block_high) + (dot(high, block_low) + dot(low, block_high))
            place = (pl.ds(k * rank, rank), pl.ds(j * half, half))
            acc[(0,) + place] += product[:, :half]
            acc[(1,) + place] += product[:, half:]

    @pl.when(step == pl.num_programs(0) - 1)
    def _():
        mine_ref[...] = acc[par_ref[0]]
        other_ref[...] = acc[1 - par_ref[0]]


def gram(parity, v, b, u, first, levels, tile):
    level_count, rows, rank = u.shape
    width = (level_count + 1) * rank // 2
    shape = jax.ShapeDtypeStruct((levels * rank, width), F32)
    whole = pl.BlockSpec((levels * rank, width), lambda i: (0, 0))
    return pl.pallas_call(
        gram_kernel,
        grid=(rows // tile,),
        out_shape=(shape, shape),
        in_specs=[
            pl.BlockSpec(memory_space=pltpu.SMEM),
            pl.BlockSpec((levels, tile, rank), lambda i: (first // levels, i, 0)),
            pl.BlockSpec((tile, rank), lambda i: (i, 0)),
            pl.BlockSpec((level_count, tile, rank), lambda i: (0, i, 0)),
        ],
        out_specs=(whole, whole),
        scratch_shapes=[pltpu.VMEM((2, levels * rank, width), F32)],
        compiler_params=pltpu.CompilerParams(vmem_limit_bytes=VMEM_LIMIT),
        cost_estimate=pl.CostEstimate(
            flops=12 * levels * rank * width * rows,
            bytes_accessed=4 * rows * rank * (levels + level_count + 1) + 8 * levels * rank * width,
            transcendentals=0,
        ),
    )(parity, v, b, u)


def solve_values(parity, own_ref, sib_ref, own_other_ref, sib_other_ref):
    half = own_other_ref.shape[1]
    width = own_ref.shape[1] - half
    own_rank = joined(parity, own_ref[:, width:], own_other_ref[...])
    sib_rank = joined(parity, sib_ref[:, width:], sib_other_ref[...])
    terms = sib_ref[:, :width] - mm(sib_rank, own_ref[:, :width])
    power = mm(sib_rank, own_rank)
    answer = terms + mm(power, terms)

    def going(state):
        count, size, _, _ = state
        return jnp.logical_and(size > SETTLED, count < MOST_SWEEPS)

    def sweep(state):
        count, _, power, answer = state
        power = mm(power, power)
        answer = answer + mm(power, answer)
        return count + 1, jnp.sum(power * power), power, answer

    state = (jnp.int32(1), jnp.sum(power * power), power, answer)
    return lax.while_loop(going, sweep, state)[3]


def solve_kernel(par_ref, own_ref, sib_ref, own_other_ref, sib_other_ref, row_ref, col_ref, col_other_ref, z_ref, next_ref):
    parity = par_ref[0]
    answer = solve_values(parity, own_ref, sib_ref, own_other_ref, sib_other_ref)
    z_ref[...] = answer
    column = joined(parity, col_ref[...], col_other_ref[...])
    next_ref[...] = row_ref[:, : answer.shape[1]] - mm(column, answer)


def top_kernel(count, par_ref, own_ref, sib_ref, own_other_ref, sib_other_ref, *refs):
    parity = par_ref[0]
    z_refs, z_other_refs, out_ref = refs[:count], refs[count : 2 * count], refs[-1]
    rank = own_ref.shape[0]
    half = own_other_ref.shape[1]
    weights = [solve_values(parity, own_ref, sib_ref, own_other_ref, sib_other_ref)]
    for k in range(1, count + 1):
        weight = z_refs[k - 1][:, :half]
        for j in range(k):
            mine = z_refs[k - 1][:, (j + 1) * half : (j + 2) * half]
            other = z_other_refs[k - 1][:, j * half : (j + 1) * half]
            weight = weight - mm(joined(parity, mine, other), weights[j])
        weights.append(weight)
    for k, weight in enumerate(weights):
        out_ref[k * rank : (k + 1) * rank, :] = weight


def small_call(kernel, shapes, parity, *arrays):
    specs = [pl.BlockSpec(memory_space=pltpu.VMEM)]
    return pl.pallas_call(
        kernel,
        out_shape=shapes,
        in_specs=[pl.BlockSpec(memory_space=pltpu.SMEM)] + specs * len(arrays),
        out_specs=jax.tree.map(lambda _: specs[0], shapes),
        compiler_params=pltpu.CompilerParams(vmem_limit_bytes=VMEM_LIMIT),
        cost_estimate=pl.CostEstimate(flops=3 * 10**9, bytes_accessed=4 * 10**6, transcendentals=0),
    )(parity, *arrays)


def apply_kernel(par_ref, b_ref, u_ref, w_ref, w_other_ref, out_ref, high, low):
    levels, _, rank = u_ref.shape

    @pl.when(pl.program_id(0) == 0)
    def _():
        high[...], low[...] = split(joined(par_ref[0], w_ref[...], w_other_ref[...]))

    total = b_ref[...]
    for k in range(levels):
        u_high, u_low = split(u_ref[k])
        rows = pl.ds(k * rank, rank)
        total = total - (
            dot(u_high, high[rows, :]) + (dot(u_high, low[rows, :]) + dot(u_low, high[rows, :]))
        )
    out_ref[...] = total


def apply(parity, b, u, w, w_other, tile):
    levels, rows, rank = u.shape
    width = b.shape[1]
    half = pl.BlockSpec(w.shape, lambda i: (0, 0))
    return pl.pallas_call(
        apply_kernel,
        grid=(rows // tile,),
        out_shape=jax.ShapeDtypeStruct(b.shape, F32),
        in_specs=[
            pl.BlockSpec(memory_space=pltpu.SMEM),
            pl.BlockSpec((tile, width), lambda i: (i, 0)),
            pl.BlockSpec((levels, tile, rank), lambda i: (0, i, 0)),
            half,
            half,
        ],
        out_specs=pl.BlockSpec((tile, width), lambda i: (i, 0)),
        scratch_shapes=[pltpu.VMEM((levels * rank, width), jnp.bfloat16)] * 2,
        compiler_params=pltpu.CompilerParams(vmem_limit_bytes=VMEM_LIMIT),
    )(parity, b, u, w, w_other)


def swap(block, even_bit, odd_bit):
    count = lax.axis_size(AXES)
    route = [(i, i ^ (1 << (odd_bit if i & 1 else even_bit))) for i in range(count)]
    return lax.ppermute(block, AXES, route)


def local(b, u, v):
    depth = lax.axis_size(AXES).bit_length() - 1
    levels, row_count, rank = u.shape
    half = rank // 2
    tile = min(512, row_count)
    parity = (lax.axis_index(AXES) & 1).reshape(1)

    own, own_far = gram(parity, v, b, u, levels - 1, 1, tile)
    own = own + swap(own_far, 0, 0)
    later, own = lax.optimization_barrier((parity, own))
    middle, middle_far = gram(later, v, b, u, levels - 2, 1, tile)
    rows = [None] * levels
    answers, answers_other = [None] * levels, [None] * levels
    low = None
    for k in range(levels - 1, -1, -1):
        width = (k + 1) * half
        sibling = depth - 1 - k
        if k < levels - 1:
            own = rows[k]
        if k == levels - 2:
            later, own = lax.optimization_barrier((parity, own))
            low, low_far = gram(later, v, b, u, 0, levels - 2, tile)
        if sibling == 2:
            cut = rank * 2 // 3 // 8 * 8
            early, late = own[:cut], own[cut:]
            early_pair, late_far = swap(early, 1, 1), swap(late, 2, 2)
            if k == levels - 2:
                early_pair, late_far, low_far = lax.optimization_barrier((early_pair, late_far, low_far))
            early = early + early_pair
            both = swap(jnp.concatenate([late, late_far], axis=0), 1, 1)
            early_far = swap(early, 2, 2)
            own = jnp.concatenate([early, late + both[: rank - cut]], axis=0)
            sib = jnp.concatenate([early_far, late_far + both[rank - cut :]], axis=0)
        else:
            for step in range(1, sibling):
                moved = swap(own, step, step % (sibling - 1) + 1)
                if k == levels - 2 and step == 1:
                    moved, low_far = lax.optimization_barrier((moved, low_far))
                own = own + moved
            sib = swap(own, sibling, sibling)
        own_other = swap(own[:, width:], 0, 0)
        if k == levels - 1:
            sib, middle_far = lax.optimization_barrier((sib, middle_far))
            middle = middle + swap(middle_far, 0, 0)
            rows[k - 1] = middle
        if k == levels - 2:
            low = low + swap(low_far, 0, 0)
            column = low[:, (k + 2) * half :]
            column = joined(parity[0], column, swap(column, 0, 0))
            z = answers[k + 1]
            low = low[:, : (k + 2) * half] - jnp.dot(
                column, z, precision=lax.Precision.HIGH, preferred_element_type=F32
            )
            for i in range(k):
                rows[i] = low[i * rank : (i + 1) * rank]
        sib_other = swap(sib[:, width:], 0, 0)
        if k > 0:
            near = [k - 1] if k == levels - 1 else list(range(k))
            cols = jnp.concatenate([rows[i][:, width : width + half] for i in near], axis=0)
            cols_other = swap(cols, 0, 0)
            last = slice((len(near) - 1) * rank, len(near) * rank)
            shape = jax.ShapeDtypeStruct((rank, width), F32)
            z, following = small_call(
                solve_kernel, (shape, shape), parity, own, sib, own_other, sib_other,
                rows[k - 1][:, :width], cols[last], cols_other[last],
            )
            answers[k] = z
            answers_other[k] = swap(z[:, half:], 0, 0)
            rows[k - 1] = following
            if len(near) > 1:
                before = slice(0, (k - 1) * rank)
                column = joined(parity[0], cols[before], cols_other[before])
                change = jnp.dot(column, z, precision=lax.Precision.HIGH, preferred_element_type=F32)
                for i in range(k - 1):
                    rows[i] = rows[i][:, :width] - change[i * rank : (i + 1) * rank]
        else:
            shape = jax.ShapeDtypeStruct((levels * rank, half), F32)
            weights = small_call(
                functools.partial(top_kernel, levels - 1), shape, parity, own, sib, own_other, sib_other,
                *answers[1:], *answers_other[1:],
            )
    return apply(parity, b, u, weights, swap(weights, 0, 0), tile)


def solution(mesh):
    return jax.shard_map(
        local,
        mesh=mesh,
        in_specs=(P(AXES, None), P(None, AXES, None), P(None, AXES, None)),
        out_specs=P(AXES, None),
        check_vma=False,
    )
```

```python
import functools

import jax
import jax.numpy as jnp
from jax import lax
from jax.experimental import pallas as pl
from jax.experimental.pallas import tpu as pltpu
from jax.sharding import PartitionSpec as P

AXES = ("leaf", "sub")
F32 = jnp.float32
VMEM_LIMIT = 56 * 1024 * 1024
SETTLED = 4e-6
MOST_SWEEPS = 12


def split(x):
    high = x.astype(jnp.bfloat16)
    return high, (x - high.astype(F32)).astype(jnp.bfloat16)


def dot(a, b):
    return jnp.dot(a, b, preferred_element_type=F32)


def mm(a, b):
    a_high, a_low = split(a)
    b_high, b_low = split(b)
    return dot(a_high, b_high) + (dot(a_high, b_low) + dot(a_low, b_high))


def joined(parity, mine, other):
    first = jnp.where(parity == 0, mine, other)
    second = jnp.where(parity == 0, other, mine)
    return jnp.concatenate([first, second], axis=1)


def gram_kernel(par_ref, v_ref, b_ref, u_ref, mine_ref, other_ref, acc):
    step = pl.program_id(0)
    levels, _, rank = v_ref.shape
    half = rank // 2

    @pl.when(step == 0)
    def _():
        acc[...] = jnp.zeros_like(acc)

    stacked = []
    for j in range(u_ref.shape[0] + 1):
        high, low = split(b_ref[...] if j == 0 else u_ref[j - 1])
        stacked.append((high, low))
    for k in range(levels):
        high, low = split(v_ref[k].T)
        for j, (block_high, block_low) in enumerate(stacked):
            product = dot(high, block_high) + (dot(high, block_low) + dot(low, block_high))
            place = (pl.ds(k * rank, rank), pl.ds(j * half, half))
            acc[(0,) + place] += product[:, :half]
            acc[(1,) + place] += product[:, half:]

    @pl.when(step == pl.num_programs(0) - 1)
    def _():
        mine_ref[...] = acc[par_ref[0]]
        other_ref[...] = acc[1 - par_ref[0]]


def gram(parity, v, b, u, first, levels, tile):
    level_count, rows, rank = u.shape
    width = (level_count + 1) * rank // 2
    shape = jax.ShapeDtypeStruct((levels * rank, width), F32)
    whole = pl.BlockSpec((levels * rank, width), lambda i: (0, 0))
    return pl.pallas_call(
        gram_kernel,
        grid=(rows // tile,),
        out_shape=(shape, shape),
        in_specs=[
            pl.BlockSpec(memory_space=pltpu.SMEM),
            pl.BlockSpec((levels, tile, rank), lambda i: (first // levels, i, 0)),
            pl.BlockSpec((tile, rank), lambda i: (i, 0)),
            pl.BlockSpec((level_count, tile, rank), lambda i: (0, i, 0)),
        ],
        out_specs=(whole, whole),
        scratch_shapes=[pltpu.VMEM((2, levels * rank, width), F32)],
        compiler_params=pltpu.CompilerParams(vmem_limit_bytes=VMEM_LIMIT),
        cost_estimate=pl.CostEstimate(
            flops=12 * levels * rank * width * rows,
            bytes_accessed=4 * rows * rank * (levels + level_count + 1) + 8 * levels * rank * width,
            transcendentals=0,
        ),
    )(parity, v, b, u)


def solve_values(parity, own_ref, sib_ref, own_other_ref, sib_other_ref):
    half = own_other_ref.shape[1]
    width = own_ref.shape[1] - half
    own_rank = joined(parity, own_ref[:, width:], own_other_ref[...])
    sib_rank = joined(parity, sib_ref[:, width:], sib_other_ref[...])
    rank = own_rank.shape[1]
    products = mm(sib_rank, jnp.concatenate([own_rank, own_ref[:, :width]], axis=1))
    power = products[:, :rank]
    answer = sib_ref[:, :width] - products[:, rank:]

    def going(state):
        count, size, _, _ = state
        return jnp.logical_and(size > SETTLED, count < MOST_SWEEPS)

    def sweep(state):
        count, _, power, answer = state
        products = mm(power, jnp.concatenate([power, answer], axis=1))
        return count + 1, jnp.sum(power * power), products[:, :rank], answer + products[:, rank:]

    state = sweep((jnp.int32(0), jnp.float32(0), power, answer))
    return lax.while_loop(going, sweep, state)[3]


def solve_kernel(par_ref, own_ref, sib_ref, own_other_ref, sib_other_ref, row_ref, col_ref, col_other_ref, z_ref, next_ref):
    parity = par_ref[0]
    answer = solve_values(parity, own_ref, sib_ref, own_other_ref, sib_other_ref)
    z_ref[...] = answer
    column = joined(parity, col_ref[...], col_other_ref[...])
    next_ref[...] = row_ref[:, : answer.shape[1]] - mm(column, answer)


def top_kernel(count, par_ref, own_ref, sib_ref, own_other_ref, sib_other_ref, *refs):
    parity = par_ref[0]
    z_refs, z_other_refs, out_ref = refs[:count], refs[count : 2 * count], refs[-1]
    rank = own_ref.shape[0]
    half = own_other_ref.shape[1]
    weights = [solve_values(parity, own_ref, sib_ref, own_other_ref, sib_other_ref)]
    for k in range(1, count + 1):
        weight = z_refs[k - 1][:, :half]
        for j in range(k):
            mine = z_refs[k - 1][:, (j + 1) * half : (j + 2) * half]
            other = z_other_refs[k - 1][:, j * half : (j + 1) * half]
            weight = weight - mm(joined(parity, mine, other), weights[j])
        weights.append(weight)
    for k, weight in enumerate(weights):
        out_ref[k * rank : (k + 1) * rank, :] = weight


def small_call(kernel, shapes, parity, *arrays):
    specs = [pl.BlockSpec(memory_space=pltpu.VMEM)]
    return pl.pallas_call(
        kernel,
        out_shape=shapes,
        in_specs=[pl.BlockSpec(memory_space=pltpu.SMEM)] + specs * len(arrays),
        out_specs=jax.tree.map(lambda _: specs[0], shapes),
        compiler_params=pltpu.CompilerParams(vmem_limit_bytes=VMEM_LIMIT),
        cost_estimate=pl.CostEstimate(flops=3 * 10**9, bytes_accessed=4 * 10**6, transcendentals=0),
    )(parity, *arrays)


def apply_kernel(par_ref, b_ref, u_ref, w_ref, w_other_ref, out_ref, high, low):
    levels, _, rank = u_ref.shape

    @pl.when(pl.program_id(0) == 0)
    def _():
        high[...], low[...] = split(joined(par_ref[0], w_ref[...], w_other_ref[...]))

    total = b_ref[...]
    for k in range(levels):
        u_high, u_low = split(u_ref[k])
        rows = pl.ds(k * rank, rank)
        total = total - (
            dot(u_high, high[rows, :]) + (dot(u_high, low[rows, :]) + dot(u_low, high[rows, :]))
        )
    out_ref[...] = total


def apply(parity, b, u, w, w_other, tile):
    levels, rows, rank = u.shape
    width = b.shape[1]
    half = pl.BlockSpec(w.shape, lambda i: (0, 0))
    return pl.pallas_call(
        apply_kernel,
        grid=(rows // tile,),
        out_shape=jax.ShapeDtypeStruct(b.shape, F32),
        in_specs=[
            pl.BlockSpec(memory_space=pltpu.SMEM),
            pl.BlockSpec((tile, width), lambda i: (i, 0)),
            pl.BlockSpec((levels, tile, rank), lambda i: (0, i, 0)),
            half,
            half,
        ],
        out_specs=pl.BlockSpec((tile, width), lambda i: (i, 0)),
        scratch_shapes=[pltpu.VMEM((levels * rank, width), jnp.bfloat16)] * 2,
        compiler_params=pltpu.CompilerParams(vmem_limit_bytes=VMEM_LIMIT),
    )(parity, b, u, w, w_other)


def swap(block, even_bit, odd_bit):
    count = lax.axis_size(AXES)
    route = [(i, i ^ (1 << (odd_bit if i & 1 else even_bit))) for i in range(count)]
    return lax.ppermute(block, AXES, route)


def local(b, u, v):
    depth = lax.axis_size(AXES).bit_length() - 1
    levels, row_count, rank = u.shape
    half = rank // 2
    tile = min(512, row_count)
    parity = (lax.axis_index(AXES) & 1).reshape(1)

    own, own_far = gram(parity, v, b, u, levels - 1, 1, tile)
    own = own + swap(own_far, 0, 0)
    later, own = lax.optimization_barrier((parity, own))
    middle, middle_far = gram(later, v, b, u, levels - 2, 1, tile)
    rows = [None] * levels
    answers, answers_other = [None] * levels, [None] * levels
    low = None
    for k in range(levels - 1, -1, -1):
        width = (k + 1) * half
        sibling = depth - 1 - k
        if k < levels - 1:
            own = rows[k]
        if k == levels - 2:
            later, own = lax.optimization_barrier((parity, own))
            low, low_far = gram(later, v, b, u, 0, levels - 2, tile)
        if sibling == 2:
            cut = rank * 2 // 3 // 8 * 8
            early, late = own[:cut], own[cut:]
            early_pair, late_far = swap(early, 1, 1), swap(late, 2, 2)
            if k == levels - 2:
                early_pair, late_far, low_far = lax.optimization_barrier((early_pair, late_far, low_far))
            early = early + early_pair
            both = swap(jnp.concatenate([late, late_far], axis=0), 1, 1)
            early_far = swap(early, 2, 2)
            own = jnp.concatenate([early, late + both[: rank - cut]], axis=0)
            sib = jnp.concatenate([early_far, late_far + both[rank - cut :]], axis=0)
        else:
            for step in range(1, sibling):
                moved = swap(own, step, step % (sibling - 1) + 1)
                if k == levels - 2 and step == 1:
                    moved, low_far = lax.optimization_barrier((moved, low_far))
                own = own + moved
            sib = swap(own, sibling, sibling)
        own_other = swap(own[:, width:], 0, 0)
        if k == levels - 1:
            sib, middle_far = lax.optimization_barrier((sib, middle_far))
            middle = middle + swap(middle_far, 0, 0)
            rows[k - 1] = middle
        if k == levels - 2:
            low = low + swap(low_far, 0, 0)
            column = low[:, (k + 2) * half :]
            column = joined(parity[0], column, swap(column, 0, 0))
            z = answers[k + 1]
            low = low[:, : (k + 2) * half] - jnp.dot(
                column, z, precision=lax.Precision.HIGH, preferred_element_type=F32
            )
            for i in range(k):
                rows[i] = low[i * rank : (i + 1) * rank]
        sib_other = swap(sib[:, width:], 0, 0)
        if k > 0:
            near = [k - 1] if k == levels - 1 else list(range(k))
            cols = jnp.concatenate([rows[i][:, width : width + half] for i in near], axis=0)
            cols_other = swap(cols, 0, 0)
            last = slice((len(near) - 1) * rank, len(near) * rank)
            shape = jax.ShapeDtypeStruct((rank, width), F32)
            z, following = small_call(
                solve_kernel, (shape, shape), parity, own, sib, own_other, sib_other,
                rows[k - 1][:, :width], cols[last], cols_other[last],
            )
            answers[k] = z
            answers_other[k] = swap(z[:, half:], 0, 0)
            rows[k - 1] = following
            if len(near) > 1:
                before = slice(0, (k - 1) * rank)
                column = joined(parity[0], cols[before], cols_other[before])
                change = jnp.dot(column, z, precision=lax.Precision.HIGH, preferred_element_type=F32)
                for i in range(k - 1):
                    rows[i] = rows[i][:, :width] - change[i * rank : (i + 1) * rank]
        else:
            shape = jax.ShapeDtypeStruct((levels * rank, half), F32)
            weights = small_call(
                functools.partial(top_kernel, levels - 1), shape, parity, own, sib, own_other, sib_other,
                *answers[1:], *answers_other[1:],
            )
    return apply(parity, b, u, weights, swap(weights, 0, 0), tile)


def solution(mesh):
    return jax.shard_map(
        local,
        mesh=mesh,
        in_specs=(P(AXES, None), P(None, AXES, None), P(None, AXES, None)),
        out_specs=P(AXES, None),
        check_vma=False,
    )
```

```python
import functools

import jax
import jax.numpy as jnp
from jax import lax
from jax.experimental import pallas as pl
from jax.experimental.pallas import tpu as pltpu
from jax.sharding import PartitionSpec as P

AXES = ("leaf", "sub")
F32 = jnp.float32
VMEM_LIMIT = 56 * 1024 * 1024
SETTLED = 4e-6
MOST_SWEEPS = 12


def split(x):
    high = x.astype(jnp.bfloat16)
    return high, (x - high.astype(F32)).astype(jnp.bfloat16)


def dot(a, b):
    return jnp.dot(a, b, preferred_element_type=F32)


def mm(a, b):
    a_high, a_low = split(a)
    b_high, b_low = split(b)
    return dot(a_high, b_high) + (dot(a_high, b_low) + dot(a_low, b_high))


def joined(parity, mine, other):
    first = jnp.where(parity == 0, mine, other)
    second = jnp.where(parity == 0, other, mine)
    return jnp.concatenate([first, second], axis=1)


def gram_kernel(par_ref, v_ref, b_ref, u_ref, mine_ref, other_ref, acc):
    step = pl.program_id(0)
    levels, _, rank = v_ref.shape
    half = rank // 2

    @pl.when(step == 0)
    def _():
        acc[...] = jnp.zeros_like(acc)

    stacked = []
    for j in range(u_ref.shape[0] + 1):
        high, low = split(b_ref[...] if j == 0 else u_ref[j - 1])
        stacked.append((high, low))
    for k in range(levels):
        high, low = split(v_ref[k].T)
        for j, (block_high, block_low) in enumerate(stacked):
            product = dot(high, block_high) + (dot(high, block_low) + dot(low, block_high))
            place = (pl.ds(k * rank, rank), pl.ds(j * half, half))
            acc[(0,) + place] += product[:, :half]
            acc[(1,) + place] += product[:, half:]

    @pl.when(step == pl.num_programs(0) - 1)
    def _():
        mine_ref[...] = acc[par_ref[0]]
        other_ref[...] = acc[1 - par_ref[0]]


def gram(parity, v, b, u, first, levels, tile):
    level_count, rows, rank = u.shape
    width = (level_count + 1) * rank // 2
    shape = jax.ShapeDtypeStruct((levels * rank, width), F32)
    whole = pl.BlockSpec((levels * rank, width), lambda i: (0, 0))
    return pl.pallas_call(
        gram_kernel,
        grid=(rows // tile,),
        out_shape=(shape, shape),
        in_specs=[
            pl.BlockSpec(memory_space=pltpu.SMEM),
            pl.BlockSpec((levels, tile, rank), lambda i: (first // levels, i, 0)),
            pl.BlockSpec((tile, rank), lambda i: (i, 0)),
            pl.BlockSpec((level_count, tile, rank), lambda i: (0, i, 0)),
        ],
        out_specs=(whole, whole),
        scratch_shapes=[pltpu.VMEM((2, levels * rank, width), F32)],
        compiler_params=pltpu.CompilerParams(vmem_limit_bytes=VMEM_LIMIT),
        cost_estimate=pl.CostEstimate(
            flops=12 * levels * rank * width * rows,
            bytes_accessed=4 * rows * rank * (levels + level_count + 1) + 8 * levels * rank * width,
            transcendentals=0,
        ),
    )(parity, v, b, u)


def solve_values(parity, own_ref, sib_ref, own_other_ref, sib_other_ref):
    half = own_other_ref.shape[1]
    width = own_ref.shape[1] - half
    own_rank = joined(parity, own_ref[:, width:], own_other_ref[...])
    sib_rank = joined(parity, sib_ref[:, width:], sib_other_ref[...])
    rank = own_rank.shape[1]
    products = mm(sib_rank, jnp.concatenate([own_rank, own_ref[:, :width]], axis=1))
    power = products[:, :rank]
    answer = sib_ref[:, :width] - products[:, rank:]

    def going(state):
        count, size, _, _ = state
        return jnp.logical_and(size > SETTLED, count < MOST_SWEEPS)

    def sweep(state):
        count, _, power, answer = state
        products = mm(power, jnp.concatenate([power, answer], axis=1))
        return count + 1, jnp.sum(power * power), products[:, :rank], answer + products[:, rank:]

    state = sweep((jnp.int32(0), jnp.float32(0), power, answer))
    return lax.while_loop(going, sweep, state)[3]


def solve_kernel(par_ref, own_ref, sib_ref, own_other_ref, sib_other_ref, row_ref, col_ref, col_other_ref, z_ref, *next_refs):
    parity = par_ref[0]
    answer = solve_values(parity, own_ref, sib_ref, own_other_ref, sib_other_ref)
    z_ref[...] = answer
    column = joined(parity, col_ref[...], col_other_ref[...])
    following = row_ref[:, : answer.shape[1]] - mm(column, answer)
    start = 0
    for next_ref in next_refs:
        next_ref[...] = following[start : start + next_ref.shape[0]]
        start += next_ref.shape[0]


def top_kernel(count, par_ref, own_ref, sib_ref, own_other_ref, sib_other_ref, *refs):
    parity = par_ref[0]
    z_refs, z_other_refs, out_ref = refs[:count], refs[count : 2 * count], refs[-1]
    rank = own_ref.shape[0]
    half = own_other_ref.shape[1]
    weights = [solve_values(parity, own_ref, sib_ref, own_other_ref, sib_other_ref)]
    for k in range(1, count + 1):
        weight = z_refs[k - 1][:, :half]
        for j in range(k):
            mine = z_refs[k - 1][:, (j + 1) * half : (j + 2) * half]
            other = z_other_refs[k - 1][:, j * half : (j + 1) * half]
            weight = weight - mm(joined(parity, mine, other), weights[j])
        weights.append(weight)
    for k, weight in enumerate(weights):
        out_ref[k * rank : (k + 1) * rank, :] = weight


def small_call(kernel, shapes, parity, *arrays):
    specs = [pl.BlockSpec(memory_space=pltpu.VMEM)]
    return pl.pallas_call(
        kernel,
        out_shape=shapes,
        in_specs=[pl.BlockSpec(memory_space=pltpu.SMEM)] + specs * len(arrays),
        out_specs=jax.tree.map(lambda _: specs[0], shapes),
        compiler_params=pltpu.CompilerParams(vmem_limit_bytes=VMEM_LIMIT),
        cost_estimate=pl.CostEstimate(flops=3 * 10**9, bytes_accessed=4 * 10**6, transcendentals=0),
    )(parity, *arrays)


def apply_kernel(par_ref, b_ref, u_ref, w_ref, w_other_ref, out_ref, high, low):
    levels, _, rank = u_ref.shape

    @pl.when(pl.program_id(0) == 0)
    def _():
        high[...], low[...] = split(joined(par_ref[0], w_ref[...], w_other_ref[...]))

    total = b_ref[...]
    for k in range(levels):
        u_high, u_low = split(u_ref[k])
        rows = pl.ds(k * rank, rank)
        total = total - (
            dot(u_high, high[rows, :]) + (dot(u_high, low[rows, :]) + dot(u_low, high[rows, :]))
        )
    out_ref[...] = total


def apply(parity, b, u, w, w_other, tile):
    levels, rows, rank = u.shape
    width = b.shape[1]
    half = pl.BlockSpec(w.shape, lambda i: (0, 0))
    return pl.pallas_call(
        apply_kernel,
        grid=(rows // tile,),
        out_shape=jax.ShapeDtypeStruct(b.shape, F32),
        in_specs=[
            pl.BlockSpec(memory_space=pltpu.SMEM),
            pl.BlockSpec((tile, width), lambda i: (i, 0)),
            pl.BlockSpec((levels, tile, rank), lambda i: (0, i, 0)),
            half,
            half,
        ],
        out_specs=pl.BlockSpec((tile, width), lambda i: (i, 0)),
        scratch_shapes=[pltpu.VMEM((levels * rank, width), jnp.bfloat16)] * 2,
        compiler_params=pltpu.CompilerParams(vmem_limit_bytes=VMEM_LIMIT),
    )(parity, b, u, w, w_other)


def swap(block, even_bit, odd_bit):
    count = lax.axis_size(AXES)
    route = [(i, i ^ (1 << (odd_bit if i & 1 else even_bit))) for i in range(count)]
    return lax.ppermute(block, AXES, route)


def local(b, u, v):
    depth = lax.axis_size(AXES).bit_length() - 1
    levels, row_count, rank = u.shape
    half = rank // 2
    tile = min(512, row_count)
    parity = (lax.axis_index(AXES) & 1).reshape(1)

    own, own_far = gram(parity, v, b, u, levels - 1, 1, tile)
    own = own + swap(own_far, 0, 0)
    later, own = lax.optimization_barrier((parity, own))
    middle, middle_far = gram(later, v, b, u, levels - 2, 1, tile)
    rows = [None] * levels
    answers, answers_other = [None] * levels, [None] * levels
    low = None
    for k in range(levels - 1, -1, -1):
        width = (k + 1) * half
        sibling = depth - 1 - k
        if k < levels - 1:
            own = rows[k]
        if k == levels - 2:
            later, own = lax.optimization_barrier((parity, own))
            low, low_far = gram(later, v, b, u, 0, levels - 2, tile)
        if sibling == 2:
            cut = rank * 2 // 3 // 8 * 8
            early, late = own if isinstance(own, list) else (own[:cut], own[cut:])
            early_pair, late_far = swap(early, 1, 1), swap(late, 2, 2)
            if k == levels - 2:
                early_pair, late_far, low_far = lax.optimization_barrier((early_pair, late_far, low_far))
            early = early + early_pair
            both = swap(jnp.concatenate([late, late_far], axis=0), 1, 1)
            early_far = swap(early, 2, 2)
            own = jnp.concatenate([early, late + both[: rank - cut]], axis=0)
            sib = jnp.concatenate([early_far, late_far + both[rank - cut :]], axis=0)
        else:
            for step in range(1, sibling):
                moved = swap(own, step, step % (sibling - 1) + 1)
                if k == levels - 2 and step == 1:
                    moved, low_far = lax.optimization_barrier((moved, low_far))
                own = own + moved
            sib = swap(own, sibling, sibling)
        own_other = swap(own[:, width:], 0, 0)
        if k == levels - 1:
            sib, middle_far = lax.optimization_barrier((sib, middle_far))
            middle = middle + swap(middle_far, 0, 0)
            rows[k - 1] = middle
        if k == levels - 2:
            low = low + swap(low_far, 0, 0)
            column = low[:, (k + 2) * half :]
            column = joined(parity[0], column, swap(column, 0, 0))
            z = answers[k + 1]
            low = low[:, : (k + 2) * half] - jnp.dot(
                column, z, precision=lax.Precision.HIGH, preferred_element_type=F32
            )
            for i in range(k):
                rows[i] = low[i * rank : (i + 1) * rank]
        sib_other = swap(sib[:, width:], 0, 0)
        if k > 0:
            near = [k - 1] if k == levels - 1 else list(range(k))
            cols = jnp.concatenate([rows[i][:, width : width + half] for i in near], axis=0)
            cols_other = swap(cols, 0, 0)
            last = slice((len(near) - 1) * rank, len(near) * rank)
            shape = jax.ShapeDtypeStruct((rank, width), F32)
            pieces = [rank]
            if sibling == 1:
                cut = rank * 2 // 3 // 8 * 8
                pieces = [cut, rank - cut]
            z, *following = small_call(
                solve_kernel, (shape, *[jax.ShapeDtypeStruct((p, width), F32) for p in pieces]), parity, own, sib, own_other, sib_other,
                rows[k - 1][:, :width], cols[last], cols_other[last],
            )
            answers[k] = z
            answers_other[k] = swap(z[:, half:], 0, 0)
            rows[k - 1] = following if len(pieces) > 1 else following[0]
            if len(near) > 1:
                before = slice(0, (k - 1) * rank)
                column = joined(parity[0], cols[before], cols_other[before])
                change = jnp.dot(column, z, precision=lax.Precision.HIGH, preferred_element_type=F32)
                for i in range(k - 1):
                    rows[i] = rows[i][:, :width] - change[i * rank : (i + 1) * rank]
        else:
            shape = jax.ShapeDtypeStruct((levels * rank, half), F32)
            weights = small_call(
                functools.partial(top_kernel, levels - 1), shape, parity, own, sib, own_other, sib_other,
                *answers[1:], *answers_other[1:],
            )
    return apply(parity, b, u, weights, swap(weights, 0, 0), tile)


def solution(mesh):
    return jax.shard_map(
        local,
        mesh=mesh,
        in_specs=(P(AXES, None), P(None, AXES, None), P(None, AXES, None)),
        out_specs=P(AXES, None),
        check_vma=False,
    )
```

```python
import functools

import jax
import jax.numpy as jnp
from jax import lax
from jax.experimental import pallas as pl
from jax.experimental.pallas import tpu as pltpu
from jax.sharding import PartitionSpec as P

AXES = ("leaf", "sub")
F32 = jnp.float32
VMEM_LIMIT = 56 * 1024 * 1024
SETTLED = 4e-6
MOST_SWEEPS = 12


def split(x):
    high = x.astype(jnp.bfloat16)
    return high, (x - high.astype(F32)).astype(jnp.bfloat16)


def dot(a, b):
    return jnp.dot(a, b, preferred_element_type=F32)


def mm(a, b):
    a_high, a_low = split(a)
    b_high, b_low = split(b)
    return dot(a_high, b_high) + (dot(a_high, b_low) + dot(a_low, b_high))


def joined(parity, mine, other):
    first = jnp.where(parity == 0, mine, other)
    second = jnp.where(parity == 0, other, mine)
    return jnp.concatenate([first, second], axis=1)


def gram_kernel(par_ref, v_ref, b_ref, u_ref, mine_ref, other_ref, acc):
    step = pl.program_id(0)
    levels, _, rank = v_ref.shape
    half = rank // 2

    @pl.when(step == 0)
    def _():
        acc[...] = jnp.zeros_like(acc)

    stacked = []
    for j in range(u_ref.shape[0] + 1):
        high, low = split(b_ref[...] if j == 0 else u_ref[j - 1])
        stacked.append((high, low))
    for k in range(levels):
        high, low = split(v_ref[k].T)
        for j, (block_high, block_low) in enumerate(stacked):
            product = dot(high, block_high) + (dot(high, block_low) + dot(low, block_high))
            place = (pl.ds(k * rank, rank), pl.ds(j * half, half))
            acc[(0,) + place] += product[:, :half]
            acc[(1,) + place] += product[:, half:]

    @pl.when(step == pl.num_programs(0) - 1)
    def _():
        mine_ref[...] = acc[par_ref[0]]
        other_ref[...] = acc[1 - par_ref[0]]


def gram(parity, v, b, u, first, levels, tile):
    level_count, rows, rank = u.shape
    width = (level_count + 1) * rank // 2
    shape = jax.ShapeDtypeStruct((levels * rank, width), F32)
    whole = pl.BlockSpec((levels * rank, width), lambda i: (0, 0))
    return pl.pallas_call(
        gram_kernel,
        grid=(rows // tile,),
        out_shape=(shape, shape),
        in_specs=[
            pl.BlockSpec(memory_space=pltpu.SMEM),
            pl.BlockSpec((levels, tile, rank), lambda i: (first // levels, i, 0)),
            pl.BlockSpec((tile, rank), lambda i: (i, 0)),
            pl.BlockSpec((level_count, tile, rank), lambda i: (0, i, 0)),
        ],
        out_specs=(whole, whole),
        scratch_shapes=[pltpu.VMEM((2, levels * rank, width), F32)],
        compiler_params=pltpu.CompilerParams(vmem_limit_bytes=VMEM_LIMIT),
        cost_estimate=pl.CostEstimate(
            flops=12 * levels * rank * width * rows,
            bytes_accessed=4 * rows * rank * (levels + level_count + 1) + 8 * levels * rank * width,
            transcendentals=0,
        ),
    )(parity, v, b, u)


def solve_values(parity, own_ref, sib_ref, own_other_ref, sib_other_ref):
    half = own_other_ref.shape[1]
    width = own_ref.shape[1] - half
    own_rank = joined(parity, own_ref[:, width:], own_other_ref[...])
    sib_rank = joined(parity, sib_ref[:, width:], sib_other_ref[...])
    rank = own_rank.shape[1]
    products = mm(sib_rank, jnp.concatenate([own_rank, own_ref[:, :width]], axis=1))
    power = products[:, :rank]
    answer = sib_ref[:, :width] - products[:, rank:]

    def going(state):
        count, size, _, _ = state
        return jnp.logical_and(size > SETTLED, count < MOST_SWEEPS)

    def sweep(state):
        count, _, power, answer = state
        products = mm(power, jnp.concatenate([power, answer], axis=1))
        return count + 1, jnp.sum(power * power), products[:, :rank], answer + products[:, rank:]

    state = sweep((jnp.int32(0), jnp.float32(0), power, answer))
    return lax.while_loop(going, sweep, state)[3]


def solve_kernel(par_ref, own_ref, sib_ref, own_other_ref, sib_other_ref, row_ref, col_ref, col_other_ref, z_ref, *next_refs):
    parity = par_ref[0]
    answer = solve_values(parity, own_ref, sib_ref, own_other_ref, sib_other_ref)
    z_ref[...] = answer
    column = joined(parity, col_ref[...], col_other_ref[...])
    following = row_ref[:, : answer.shape[1]] - mm(column, answer)
    start = 0
    for next_ref in next_refs:
        next_ref[...] = following[start : start + next_ref.shape[0]]
        start += next_ref.shape[0]


def top_kernel(count, par_ref, own_ref, sib_ref, own_other_ref, sib_other_ref, *refs):
    parity = par_ref[0]
    z_refs, z_other_refs, out_ref = refs[:count], refs[count : 2 * count], refs[-1]
    rank = own_ref.shape[0]
    half = own_other_ref.shape[1]
    weights = [solve_values(parity, own_ref, sib_ref, own_other_ref, sib_other_ref)]
    for k in range(1, count + 1):
        weight = z_refs[k - 1][:, :half]
        for j in range(k):
            mine = z_refs[k - 1][:, (j + 1) * half : (j + 2) * half]
            other = z_other_refs[k - 1][:, j * half : (j + 1) * half]
            weight = weight - mm(joined(parity, mine, other), weights[j])
        weights.append(weight)
    for k, weight in enumerate(weights):
        out_ref[k * rank : (k + 1) * rank, :] = weight


def small_call(kernel, shapes, parity, *arrays):
    specs = [pl.BlockSpec(memory_space=pltpu.VMEM)]
    return pl.pallas_call(
        kernel,
        out_shape=shapes,
        in_specs=[pl.BlockSpec(memory_space=pltpu.SMEM)] + specs * len(arrays),
        out_specs=jax.tree.map(lambda _: specs[0], shapes),
        compiler_params=pltpu.CompilerParams(vmem_limit_bytes=VMEM_LIMIT),
        cost_estimate=pl.CostEstimate(flops=3 * 10**9, bytes_accessed=4 * 10**6, transcendentals=0),
    )(parity, *arrays)


def apply_kernel(par_ref, b_ref, u_ref, w_ref, w_other_ref, out_ref, high, low):
    levels = u_ref.shape[0]

    @pl.when(pl.program_id(0) == 0)
    def _():
        high[...], low[...] = split(joined(par_ref[0], w_ref[...], w_other_ref[...]))

    parts = [split(u_ref[k]) for k in range(levels)]
    u_high = jnp.concatenate([part[0] for part in parts], axis=1)
    u_low = jnp.concatenate([part[1] for part in parts], axis=1)
    total = b_ref[...] - (
        dot(u_high, high[...]) + (dot(u_high, low[...]) + dot(u_low, high[...]))
    )
    out_ref[...] = total


def apply(parity, b, u, w, w_other, tile):
    levels, rows, rank = u.shape
    width = b.shape[1]
    half = pl.BlockSpec(w.shape, lambda i: (0, 0))
    return pl.pallas_call(
        apply_kernel,
        grid=(rows // tile,),
        out_shape=jax.ShapeDtypeStruct(b.shape, F32),
        in_specs=[
            pl.BlockSpec(memory_space=pltpu.SMEM),
            pl.BlockSpec((tile, width), lambda i: (i, 0)),
            pl.BlockSpec((levels, tile, rank), lambda i: (0, i, 0)),
            half,
            half,
        ],
        out_specs=pl.BlockSpec((tile, width), lambda i: (i, 0)),
        scratch_shapes=[pltpu.VMEM((levels * rank, width), jnp.bfloat16)] * 2,
        compiler_params=pltpu.CompilerParams(vmem_limit_bytes=VMEM_LIMIT),
    )(parity, b, u, w, w_other)


def swap(block, even_bit, odd_bit):
    count = lax.axis_size(AXES)
    route = [(i, i ^ (1 << (odd_bit if i & 1 else even_bit))) for i in range(count)]
    return lax.ppermute(block, AXES, route)


def local(b, u, v):
    depth = lax.axis_size(AXES).bit_length() - 1
    levels, row_count, rank = u.shape
    half = rank // 2
    tile = min(512, row_count)
    parity = (lax.axis_index(AXES) & 1).reshape(1)

    own, own_far = gram(parity, v, b, u, levels - 1, 1, tile)
    own = own + swap(own_far, 0, 0)
    later, own = lax.optimization_barrier((parity, own))
    middle, middle_far = gram(later, v, b, u, levels - 2, 1, tile)
    rows = [None] * levels
    answers, answers_other = [None] * levels, [None] * levels
    low = None
    for k in range(levels - 1, -1, -1):
        width = (k + 1) * half
        sibling = depth - 1 - k
        if k < levels - 1:
            own = rows[k]
        if k == levels - 2:
            later, own = lax.optimization_barrier((parity, own))
            low, low_far = gram(later, v, b, u, 0, levels - 2, tile)
        if sibling == 2:
            cut = rank * 2 // 3 // 8 * 8
            early, late = own if isinstance(own, list) else (own[:cut], own[cut:])
            early_pair, late_far = swap(early, 1, 1), swap(late, 2, 2)
            if k == levels - 2:
                early_pair, late_far, low_far = lax.optimization_barrier((early_pair, late_far, low_far))
            early = early + early_pair
            both = swap(jnp.concatenate([late, late_far], axis=0), 1, 1)
            early_far = swap(early, 2, 2)
            own = jnp.concatenate([early, late + both[: rank - cut]], axis=0)
            sib = jnp.concatenate([early_far, late_far + both[rank - cut :]], axis=0)
        else:
            for step in range(1, sibling):
                moved = swap(own, step, step % (sibling - 1) + 1)
                if k == levels - 2 and step == 1:
                    moved, low_far = lax.optimization_barrier((moved, low_far))
                own = own + moved
            sib = swap(own, sibling, sibling)
        own_other = swap(own[:, width:], 0, 0)
        if k == levels - 1:
            sib, middle_far = lax.optimization_barrier((sib, middle_far))
            middle = middle + swap(middle_far, 0, 0)
            rows[k - 1] = middle
        if k == levels - 2:
            low = low + swap(low_far, 0, 0)
            column = low[:, (k + 2) * half :]
            column = joined(parity[0], column, swap(column, 0, 0))
            z = answers[k + 1]
            low = low[:, : (k + 2) * half] - jnp.dot(
                column, z, precision=lax.Precision.HIGH, preferred_element_type=F32
            )
            for i in range(k):
                rows[i] = low[i * rank : (i + 1) * rank]
        sib_other = swap(sib[:, width:], 0, 0)
        if k > 0:
            near = [k - 1] if k == levels - 1 else list(range(k))
            cols = jnp.concatenate([rows[i][:, width : width + half] for i in near], axis=0)
            cols_other = swap(cols, 0, 0)
            last = slice((len(near) - 1) * rank, len(near) * rank)
            shape = jax.ShapeDtypeStruct((rank, width), F32)
            pieces = [rank]
            if sibling == 1:
                cut = rank * 2 // 3 // 8 * 8
                pieces = [cut, rank - cut]
            z, *following = small_call(
                solve_kernel, (shape, *[jax.ShapeDtypeStruct((p, width), F32) for p in pieces]), parity, own, sib, own_other, sib_other,
                rows[k - 1][:, :width], cols[last], cols_other[last],
            )
            answers[k] = z
            answers_other[k] = swap(z[:, half:], 0, 0)
            rows[k - 1] = following if len(pieces) > 1 else following[0]
            if len(near) > 1:
                before = slice(0, (k - 1) * rank)
                column = joined(parity[0], cols[before], cols_other[before])
                change = jnp.dot(column, z, precision=lax.Precision.HIGH, preferred_element_type=F32)
                for i in range(k - 1):
                    rows[i] = rows[i][:, :width] - change[i * rank : (i + 1) * rank]
        else:
            shape = jax.ShapeDtypeStruct((levels * rank, half), F32)
            weights = small_call(
                functools.partial(top_kernel, levels - 1), shape, parity, own, sib, own_other, sib_other,
                *answers[1:], *answers_other[1:],
            )
    return apply(parity, b, u, weights, swap(weights, 0, 0), tile)


def solution(mesh):
    return jax.shard_map(
        local,
        mesh=mesh,
        in_specs=(P(AXES, None), P(None, AXES, None), P(None, AXES, None)),
        out_specs=P(AXES, None),
        check_vma=False,
    )
```
